512 devices in a mesh: dp: 16 (over y, z_hi), ctx: 32 (over z_lo, x, core).
Axes of the slice: x: 4, y: 8, z: 8 (z_hi: 2, z_lo: 4; z = z_hi * 4 + z_lo), core: 2. Of those that a mesh axis runs over, the one named last changes fastest.
Arguments:
- queries: bfloat16 [16, 8192, 512], P('dp', 'ctx'), may hold values from -6 to 6
- keys: bfloat16 [16, 8192, 512], P('dp', 'ctx'), may hold values from -6 to 6
- values: bfloat16 [16, 8192, 512], P('dp', 'ctx'), may hold values from -24 to 24
- out_grad: bfloat16 [16, 8192, 1024], P('dp', 'ctx'), may hold values from -6 to 6
- w_out: bfloat16 [512, 1024], replicated, may hold values from -0.25 to 0.25
- block_mask: int32 [16, 64, 3], P('dp'), may hold values 0 or 1
Outputs:
- output: bfloat16 [16, 8192, 1024], P('dp', 'ctx')
- query_grad: bfloat16 [16, 8192, 512], P('dp', 'ctx')
- key_grad: bfloat16 [16, 8192, 512], P('dp', 'ctx')
- value_grad: bfloat16 [16, 8192, 512], P('dp', 'ctx')
- weight_grad: float32 [512, 1024], P('ctx')
The draws below stay inside these ranges and needn't reach their ends.
All inputs are finite; a program needn't handle non-finite values. No bound on the sum of `block_mask` on one device may be relied on, other than what follows from the above.
Results may differ from the reference program's by a relative error of at most 0.038.
Values may be sent and summed in bfloat16 or wider, within the bound.
A program may use at most 64 MiB of HBM per device.

```python
import jax
import jax.numpy as jnp
from jax import lax

D = 1024
HEADS = 8
HD = 64
BLK = 128
RAD = 1
DA = 512
CAND = 3
TOKENS = 8192
NBLK = 64
VOLUMES = 16


def draw_queries(key, part):
    own_key = jax.random.fold_in(key, 1)
    dims_all = (VOLUMES, TOKENS, DA)
    return (1.5 * jax.random.truncated_normal(own_key, -4.0, 4.0, dims_all, jnp.float32)).astype(jnp.bfloat16)


def draw_keys(key, part):
    own_key = jax.random.fold_in(key, 2)
    dims_all = (VOLUMES, TOKENS, DA)
    return jax.random.truncated_normal(own_key, -6.0, 6.0, dims_all, jnp.float32).astype(jnp.bfloat16)


def place_ends(values, stream_key, smallest, top_value):
    index_at = [jax.random.randint(jax.random.fold_in(stream_key, axis), (), 0, length) for axis, length in enumerate(values.shape)]
    longest = values.shape.index(max(values.shape))
    next_to = index_at[:longest] + [(index_at[longest] + 1) % values.shape[longest]] + index_at[longest + 1:]
    return values.at[tuple(index_at)].set(smallest).at[tuple(next_to)].set(top_value)


def shard_levels(stream_key, dims, cuts, low, top_value):
    def one(axis_at, blocks):
        draws = jax.random.uniform(jax.random.fold_in(jax.random.fold_in(stream_key, 6), axis_at), (blocks,), jnp.float32, low / len(cuts), top_value / len(cuts))
        return jnp.repeat(jnp.exp(draws), dims[axis_at] // blocks).reshape((-1,) + (1,) * (len(dims) - axis_at - 1))

    level = one(*cuts[0])
    for cut in cuts[1:]:
        level = level * one(*cut)
    return level


def scatter_about(rng, shape, spread, limit, pieces=(), held_as=jnp.bfloat16):
    values = spread * jax.random.normal(rng, shape, jnp.float32)
    if pieces:
        values = values * shard_levels(rng, shape, pieces, -0.22, 0.18)
    return jnp.clip(values, -limit, limit).astype(held_as)


def setup_inputs(seed: int = 0) -> dict:
    splits = jax.random.split(jax.random.key(seed), 7)
    return {
        "queries": draw_queries(jax.random.fold_in(splits[6], 71), 0),
        "keys": draw_keys(jax.random.fold_in(splits[6], 71), 0),
        "values": scatter_about(splits[2], (VOLUMES, TOKENS, DA), 4.0, 24.0, ((0, 16), (1, 32))),
        "out_grad": scatter_about(splits[3], (VOLUMES, TOKENS, D), 1.0, 6.0, ((0, 16), (1, 32))),
        "w_out": scatter_about(splits[4], (DA, D), DA ** -0.5, 0.25),
        "block_mask": place_ends((jax.random.randint(splits[5], (VOLUMES, NBLK, CAND), 0, 5) < 3).astype(jnp.int32), jax.random.fold_in(splits[5], 1), 0, 1),
    }


big_negative = -1e30


def allowed_keys(mask_row):
    centre = jnp.arange(2 * RAD + 1) == RAD
    allowed = (mask_row == 1) | centre
    return jnp.repeat(allowed, BLK)


def one_volume(query_rows, key_rows, value_rows, grad_rows, w_out, pattern):
    rim_rows = RAD * BLK
    span_rows = (2 * RAD + 1) * BLK
    score_scale = HD ** -0.5
    key_pad = jnp.concatenate([key_rows[-rim_rows:], key_rows, key_rows[:rim_rows]], axis=0)
    value_pad = jnp.concatenate([value_rows[-rim_rows:], value_rows, value_rows[:rim_rows]], axis=0)

    def step(carry, row_block):
        key_acc, value_acc, weight_acc = carry
        first_row = (row_block * BLK).astype(jnp.int32)
        q_block = lax.dynamic_slice_in_dim(query_rows, first_row, BLK, 0)
        g_block = lax.dynamic_slice_in_dim(grad_rows, first_row, BLK, 0)
        k_window = lax.dynamic_slice_in_dim(key_pad, first_row, span_rows, 0)
        v_window = lax.dynamic_slice_in_dim(value_pad, first_row, span_rows, 0)
        allowed = allowed_keys(lax.dynamic_index_in_dim(pattern, row_block, 0, keepdims=False))
        q_heads = q_block.astype(jnp.float32).reshape(BLK, HEADS, HD)
        k_heads = k_window.astype(jnp.float32).reshape(span_rows, HEADS, HD)
        v_heads = v_window.astype(jnp.float32).reshape(span_rows, HEADS, HD)
        scores = jnp.einsum("qhd,khd->hqk", q_heads, k_heads) * score_scale
        scores = jnp.where(allowed[None, None, :], scores, big_negative)
        row_max = jnp.max(scores, axis=-1, keepdims=True)
        log_total = row_max + jnp.log(jnp.sum(jnp.exp(scores - row_max), axis=-1, keepdims=True))
        probs = jnp.exp(scores - log_total)
        probs_bf = lax.optimization_barrier(probs.astype(jnp.bfloat16)).astype(jnp.float32)
        attn_block = jnp.einsum("hqk,khd->qhd", probs_bf, v_heads).reshape(BLK, HEADS * HD).astype(jnp.bfloat16)
        out_block = jnp.dot(attn_block, w_out, preferred_element_type=jnp.float32).astype(jnp.bfloat16)
        attn_grad = lax.dot_general(g_block, w_out, (((1,), (1,)), ((), ())), preferred_element_type=jnp.float32).astype(jnp.bfloat16)
        grad_heads = attn_grad.astype(jnp.float32).reshape(BLK, HEADS, HD)
        row_delta = jnp.sum(grad_heads * attn_block.astype(jnp.float32).reshape(BLK, HEADS, HD), axis=-1).T
        dprob = jnp.einsum("qhd,khd->hqk", grad_heads, v_heads)
        dscore = (probs * (dprob - row_delta[:, :, None]) * score_scale).astype(jnp.bfloat16)
        dscore = lax.optimization_barrier(dscore).astype(jnp.float32)
        query_block = jnp.einsum("hqk,khd->qhd", dscore, k_heads).reshape(BLK, HEADS * HD).astype(jnp.bfloat16)
        key_window = jnp.einsum("hqk,qhd->khd", dscore, q_heads).reshape(span_rows, HEADS * HD)
        value_window = jnp.einsum("hqk,qhd->khd", probs_bf, grad_heads).reshape(span_rows, HEADS * HD)
        key_acc = lax.dynamic_update_slice_in_dim(key_acc, lax.dynamic_slice_in_dim(key_acc, first_row, span_rows, 0) + key_window, first_row, 0)
        value_acc = lax.dynamic_update_slice_in_dim(value_acc, lax.dynamic_slice_in_dim(value_acc, first_row, span_rows, 0) + value_window, first_row, 0)
        weight_acc = weight_acc + lax.dot_general(attn_block, g_block, (((0,), (0,)), ((), ())), preferred_element_type=jnp.float32)
        return (key_acc, value_acc, weight_acc), (out_block, query_block)

    start_acc = jnp.zeros((TOKENS + 2 * rim_rows, HEADS * HD), jnp.float32)
    start_weight = jnp.zeros((HEADS * HD, D), jnp.float32)
    (key_acc, value_acc, weight_acc), (out_rows, query_out) = lax.scan(step, (start_acc, start_acc, start_weight), jnp.arange(NBLK, dtype=jnp.int32))

    def fold(acc):
        own_sums = acc[rim_rows:rim_rows + TOKENS]
        own_sums = own_sums.at[TOKENS - rim_rows:].add(acc[:rim_rows])
        own_sums = own_sums.at[:rim_rows].add(acc[rim_rows + TOKENS:])
        return own_sums.astype(jnp.bfloat16)

    return out_rows.reshape(TOKENS, D), query_out.reshape(TOKENS, HEADS * HD), fold(key_acc), fold(value_acc), weight_acc


def reference(queries, keys, values, out_grad, w_out, block_mask):
    def per_volume(weight_sum, items):
        query_rows, key_rows, value_rows, grad_rows, pattern = items
        out_rows, query_out, key_out, value_out, weight_acc = one_volume(query_rows, key_rows, value_rows, grad_rows, w_out, pattern)
        return weight_sum + weight_acc, (out_rows, query_out, key_out, value_out)

    weight_sum, stacked = lax.scan(per_volume, jnp.zeros((HEADS * HD, D), jnp.float32), (queries, keys, values, out_grad, block_mask))
    weight_grad = weight_sum * (VOLUMES * TOKENS) ** -0.5
    return (stacked[0], stacked[1], stacked[2], stacked[3], weight_grad)
```

```python
import functools

import jax
import jax.numpy as jnp
from jax import lax
from jax.experimental import pallas as pl
from jax.experimental.pallas import tpu as pltpu
from jax.sharding import PartitionSpec as P

HD = 64
BLK = 128
GW = 2 * HD
NG = 4
WIN = 3 * BLK
BF = jnp.bfloat16
F32 = jnp.float32
MESH = pl.DeviceIdType.MESH
NEG = -1e30


def nn(a, b):
    return lax.dot_general(a, b, (((1,), (0,)), ((), ())), preferred_element_type=F32)


def nt(a, b):
    return lax.dot_general(a, b, (((1,), (1,)), ((), ())), preferred_element_type=F32)


def block_diag(rows):
    lane = lax.broadcasted_iota(jnp.int32, rows.shape, 1)
    zero = jnp.zeros_like(rows)
    return jnp.concatenate([jnp.where(lane < HD, rows, zero), jnp.where(lane < HD, zero, rows)], axis=0)


def diagonal(both):
    return jnp.concatenate([both[:HD, :BLK], both[HD:, BLK:]], axis=0)


def kernel(
    dims, wscale,
    q_hbm, k_hbm, v_hbm, g_hbm, w_hbm, mask,
    out_s, dq_s, dk_s, dv_s, dw_out,
    q_s, k_ext, v_ext, g_s, w_s, k_t, v_t, da_t, qbd, abd, p_t, at, dw_own,
    csend, crecv, xsend, xrecv, ysend, yrecv, zsend, zrecv,
    dk_acc, dv_acc, gsend, grecv, dq_t,
    lsem, h_s, h_r, c_s, c_r, x_s, x_r, y_s, y_r, z_s, z_r, a_s, a_r, g_ss, g_rs,
):
    NY, ZH, ZL, NX = dims
    NZ = ZL * ZH
    CTX = ZL * NX * 2
    dp = lax.axis_index("dp")
    ctx = lax.axis_index("ctx")
    y, zh = dp // ZH, dp % ZH
    zl, x, core = ctx // (NX * 2), (ctx // 2) % NX, ctx % 2
    z = zh * ZL + zl

    def ident(y_, z_, x_, c_):
        return (y_ * ZH + z_ // ZL, (z_ % ZL) * (NX * 2) + x_ * 2 + c_)

    right = (dp, (ctx + 1) % CTX)
    left = (dp, (ctx + CTX - 1) % CTX)
    mate = (dp, ctx + 1 - 2 * core)
    x_peer = [ident(y, z, (x + d) % NX, core) for d in range(1, NX)]
    y_peer = [ident((y + d) % NY, z, x, core) for d in range(1, NY)]
    z_peer = [ident(y, (z + d) % NZ, x, core) for d in range(1, NZ)]

    def remote(src, dst, ssem, rsem, dev):
        return pltpu.make_async_remote_copy(
            src_ref=src, dst_ref=dst, send_sem=ssem, recv_sem=rsem, device_id=dev, device_id_type=MESH
        )

    barrier = pltpu.get_barrier_semaphore()
    peers = [right, left] + x_peer + y_peer + z_peer
    for dev in peers:
        pl.semaphore_signal(barrier, inc=1, device_id=dev, device_id_type=MESH)

    own = pl.ds(BLK, 2 * BLK)
    load_g = pltpu.make_async_copy(g_hbm, g_s, lsem.at[0])
    load_w = pltpu.make_async_copy(w_hbm, w_s, lsem.at[1])
    load_q = pltpu.make_async_copy(q_hbm, q_s, lsem.at[2])
    load_k = pltpu.make_async_copy(k_hbm, k_ext.at[own], lsem.at[3])
    load_v = pltpu.make_async_copy(v_hbm, v_ext.at[own], lsem.at[4])
    loads = [load_g, load_w, load_q, load_k, load_v]
    for copy in loads:
        copy.start()

    pl.semaphore_wait(barrier, len(peers))

    first, last = pl.ds(0, BLK), pl.ds(BLK, BLK)
    low, high = pl.ds(0, BLK), pl.ds(3 * BLK, BLK)
    halo = [
        remote(k_hbm.at[last], k_ext.at[low], h_s.at[0], h_r.at[0], right),
        remote(k_hbm.at[first], k_ext.at[high], h_s.at[1], h_r.at[1], left),
        remote(v_hbm.at[last], v_ext.at[low], h_s.at[2], h_r.at[2], right),
        remote(v_hbm.at[first], v_ext.at[high], h_s.at[3], h_r.at[3], left),
    ]
    for copy in halo:
        copy.start()

    def cols(g):
        return slice(g * GW, (g + 1) * GW)

    load_g.wait()
    load_w.wait()
    da = nt(g_s[...], w_s[...]).astype(BF)
    for b in range(2):
        for g in range(NG):
            abd[b, g] = block_diag(da[b * BLK:(b + 1) * BLK, cols(g)])
    da_t[...] = nt(w_s[...], g_s[...]).astype(BF)
    load_q.wait()
    for b in range(2):
        for g in range(NG):
            scaled = q_s[b * BLK:(b + 1) * BLK, cols(g)] * jnp.asarray(HD ** -0.5, BF)
            qbd[b, g] = block_diag(scaled)
    load_k.wait()
    load_v.wait()
    k_t[:, BLK:3 * BLK] = k_ext[BLK:3 * BLK, :].T
    v_t[:, BLK:3 * BLK] = v_ext[BLK:3 * BLK, :].T

    bias = []
    for b in range(2):
        row = ctx * 2 + b
        bias.append([jnp.where(mask[c, row] == 1, 0.0, NEG).astype(F32) for c in (0, 2)])

    for copy in halo:
        copy.wait_recv()
    k_t[:, :BLK] = k_ext[:BLK, :].T
    k_t[:, 3 * BLK:] = k_ext[3 * BLK:, :].T
    v_t[:, :BLK] = v_ext[:BLK, :].T
    v_t[:, 3 * BLK:] = v_ext[3 * BLK:, :].T

    def window(b):
        return slice(b * BLK, b * BLK + WIN)

    def forward(g):
        parts = []
        for b in range(2):
            s = nt(k_ext[window(b), cols(g)], qbd[b, g])
            lo, mid, hi = s[:BLK], s[BLK:2 * BLK], s[2 * BLK:]
            b_lo, b_hi = bias[b]
            top = jnp.maximum(
                jnp.max(mid, axis=0, keepdims=True),
                jnp.maximum(jnp.max(lo, axis=0, keepdims=True) + b_lo, jnp.max(hi, axis=0, keepdims=True) + b_hi),
            )
            e_lo = jnp.exp(lo - (top - b_lo))
            e_mid = jnp.exp(mid - top)
            e_hi = jnp.exp(hi - (top - b_hi))
            total = jnp.sum(e_lo + e_mid + e_hi, axis=0, keepdims=True)
            inv = 1.0 / total
            p = jnp.concatenate([(e_lo * inv).astype(BF), (e_mid * inv).astype(BF), (e_hi * inv).astype(BF)], axis=0)
            p_t[b, g] = p
            parts.append(diagonal(nn(v_t[cols(g), window(b)], p)).astype(BF))
        rows = jnp.concatenate(parts, axis=1)
        at[g] = rows.reshape(4, 2, 16, 2 * BLK)

    def core_copy(g):
        return remote(csend.at[g], crecv.at[g], c_s.at[g], c_r.at[g], mate)

    def x_copy(g, d):
        return remote(xsend.at[g, (x + d) % NX], xrecv.at[g, d - 1], x_s.at[g, d - 1], x_r.at[g, d - 1], x_peer[d - 1])

    def y_copy(g, d):
        return remote(ysend.at[g, (y + d) % NY], yrecv.at[g, d - 1], y_s.at[g, d - 1], y_r.at[g, d - 1], y_peer[d - 1])

    def z_copy(d):
        return remote(zsend.at[(z + d) % ZL], zrecv.at[d - 1], z_s.at[d - 1], z_r.at[d - 1], z_peer[d - 1])

    own_cols = pl.ds(pl.multiple_of(y * BLK, BLK), BLK)

    def a_copy(d):
        return remote(dw_out.at[:, own_cols], dw_out.at[:, own_cols], a_s.at[d - 1], a_r.at[d - 1], y_peer[d - 1])

    def a_arrival(d):
        there = pl.ds(pl.multiple_of(((y + NY - d) % NY) * BLK, BLK), BLK)
        return remote(dw_out.at[:, own_cols], dw_out.at[:, there], a_s.at[d - 1], a_r.at[d - 1], y_peer[d - 1])

    def weight_part(g):
        mine = at[g, :, core].reshape(64, 2 * BLK)
        other = at[g, :, 1 - core].reshape(64, 2 * BLK)
        part = nn(jnp.concatenate([mine, other], axis=0), g_s[...])
        csend[g] = part[64:].astype(BF)
        dw_own[g] = part[:64]
        core_copy(g).start()

    def core_sum(g):
        core_copy(g).wait_recv()
        total = dw_own[g] + crecv[g].astype(F32)
        xsend[g] = total.astype(BF).reshape(4, 16, 1024)
        for d in range(1, NX):
            x_copy(g, d).start()

    def x_sum(g):
        total = xsend[g, x].astype(F32)
        for d in range(1, NX):
            x_copy(g, d).wait_recv()
            total += xrecv[g, d - 1].astype(F32)
        total = total.astype(BF)
        for j in range(8):
            ysend[g, j] = total[:, j * BLK:(j + 1) * BLK]
        for d in range(1, NY):
            y_copy(g, d).start()

    def y_sum(g):
        total = ysend[g, y].astype(F32)
        for d in range(1, NY):
            y_copy(g, d).wait_recv()
            total += yrecv[g, d - 1].astype(F32)
        zsend[g] = total

    def z_start():
        for d in range(1, NZ):
            z_copy(d).start()

    def z_sum():
        total = zsend[z % ZL]
        for d in range(1, NZ):
            z_copy(d).wait_recv()
            total += zrecv[d - 1]
        dw_out[:, own_cols] = total * wscale
        for d in range(1, NY):
            a_copy(d).start()

    def grad_copy(side, g):
        return remote(gsend.at[side, g], grecv.at[side, g], g_ss.at[side, g], g_rs.at[side, g], right if side else left)

    def backward(g):
        tok = [slice(0, BLK), slice(BLK, 2 * BLK)]
        k_win, v_win = [], []
        rows = at[g].reshape(GW, 2 * BLK)
        q_parts = []
        for b in range(2):
            prod = rows[:, tok[b]].astype(F32) * da_t[cols(g), tok[b]].astype(F32)
            delta = jnp.concatenate(
                [jnp.sum(prod[:HD], axis=0, keepdims=True), jnp.sum(prod[HD:], axis=0, keepdims=True)], axis=1
            )
            dp_t = nt(v_ext[window(b), cols(g)], abd[b, g])
            p = p_t[b, g]
            ds = (p.astype(F32) * (dp_t - delta)).astype(BF)
            v_win.append(nn(p, abd[b, g]))
            k_win.append(nn(ds, qbd[b, g]))
            q_parts.append((diagonal(nn(k_t[cols(g), window(b)], ds)) * (HD ** -0.5)).astype(BF))
        for n, win in enumerate((k_win, v_win)):
            gsend[0, g, n] = win[0][:BLK].astype(BF)
            gsend[1, g, n] = win[1][2 * BLK:].astype(BF)
        grad_copy(0, g).start()
        grad_copy(1, g).start()
        dk_acc[g] = k_win[0][BLK:] + k_win[1][:2 * BLK]
        dv_acc[g] = v_win[0][BLK:] + v_win[1][:2 * BLK]
        dq_t[cols(g), :] = jnp.concatenate(q_parts, axis=1)

    for g in range(NG):
        forward(g)
        weight_part(g)
        if g >= 1:
            core_sum(g - 1)
    for g in range(NG):
        backward(g)
        if g == 0:
            core_sum(NG - 1)
        x_sum(g)
        if g >= 1:
            y_sum(g - 1)

    dq_s[...] = dq_t[...].T
    y_sum(NG - 1)
    z_start()
    attn = at[...].reshape(NG * GW, 2 * BLK).T
    out_s[...] = nn(attn, w_s[...]).astype(BF)
    z_sum()
    for g in range(NG):
        grad_copy(0, g).wait_recv()
        grad_copy(1, g).wait_recv()
        for n, (acc, dst) in enumerate(((dk_acc, dk_s), (dv_acc, dv_s))):
            dst[:BLK, cols(g)] = (acc[g, :BLK] + grecv[1, g, n].astype(F32)).astype(BF)
            dst[BLK:, cols(g)] = (acc[g, BLK:] + grecv[0, g, n].astype(F32)).astype(BF)
    for d in range(1, NY):
        a_arrival(d).wait_recv()

    for copy in halo:
        copy.wait_send()
    for g in range(NG):
        core_copy(g).wait_send()
        for d in range(1, NX):
            x_copy(g, d).wait_send()
        for d in range(1, NY):
            y_copy(g, d).wait_send()
        grad_copy(0, g).wait_send()
        grad_copy(1, g).wait_send()
    for d in range(1, NZ):
        z_copy(d).wait_send()
    for d in range(1, NY):
        a_copy(d).wait_send()


def body(dims, wscale, queries, keys, values, out_grad, w_out, block_mask):
    NY, ZH, ZL, NX = dims
    NZ = ZL * ZH
    tok, feat = queries.shape[1:]
    width = w_out.shape[1]
    hbm = pl.BlockSpec(memory_space=pl.ANY)
    vm = pltpu.VMEM
    dma = pltpu.SemaphoreType.DMA
    nx, ny, nz = max(NX - 1, 1), max(NY - 1, 1), max(NZ - 1, 1)
    outs = pl.pallas_call(
        functools.partial(kernel, dims, wscale),
        out_shape=(
            jax.ShapeDtypeStruct((tok, width), BF),
            jax.ShapeDtypeStruct((tok, feat), BF),
            jax.ShapeDtypeStruct((tok, feat), BF),
            jax.ShapeDtypeStruct((tok, feat), BF),
            jax.ShapeDtypeStruct((16, width), F32),
        ),
        in_specs=[hbm] * 5 + [pl.BlockSpec(memory_space=pltpu.SMEM)],
        out_specs=[pl.BlockSpec(memory_space=pltpu.VMEM)] * 5,
        scratch_shapes=[
            vm((tok, feat), BF),
            vm((4 * BLK, feat), BF),
            vm((4 * BLK, feat), BF),
            vm((tok, width), BF),
            vm((feat, width), BF),
            vm((feat, 4 * BLK), BF),
            vm((feat, 4 * BLK), BF),
            vm((feat, tok), BF),
            vm((2, NG, 2 * BLK, GW), BF),
            vm((2, NG, 2 * BLK, GW), BF),
            vm((2, NG, WIN, 2 * BLK), BF),
            vm((NG, 4, 2, 16, tok), BF),
            vm((NG, 64, width), F32),
            vm((NG, 64, width), BF),
            vm((NG, 64, width), BF),
            vm((NG, 4, 16, width), BF),
            vm((NG, nx, 16, width), BF),
            vm((NG, 8, 16, BLK), BF),
            vm((NG, ny, 16, BLK), BF),
            vm((NG, 16, BLK), F32),
            vm((nz, 16, BLK), F32),
            vm((NG, tok, GW), F32),
            vm((NG, tok, GW), F32),
            vm((2, NG, 2, BLK, GW), BF),
            vm((2, NG, 2, BLK, GW), BF),
            vm((feat, tok), BF),
            dma((5,)),
            dma((4,)), dma((4,)),
            dma((NG,)), dma((NG,)),
            dma((NG, nx)), dma((NG, nx)),
            dma((NG, ny)), dma((NG, ny)),
            dma((nz,)), dma((nz,)),
            dma((ny,)), dma((ny,)),
            dma((2, NG)), dma((2, NG)),
        ],
        compiler_params=pltpu.CompilerParams(
            collective_id=0, has_side_effects=True, vmem_limit_bytes=60 * 1024 * 1024
        ),
    )(queries[0], keys[0], values[0], out_grad[0], w_out, block_mask[0].T)
    return (outs[0][None], outs[1][None], outs[2][None], outs[3][None], outs[4])


def solution(mesh, dims=(8, 2, 4, 4)):
    tokens = mesh.shape["dp"] * mesh.shape["ctx"] * 256
    placed = (
        P("dp", "ctx", None),
        P("dp", "ctx", None),
        P("dp", "ctx", None),
        P("dp", "ctx", None),
        P(),
        P("dp", None, None),
    )
    return jax.shard_map(
        functools.partial(body, dims, tokens ** -0.5),
        mesh=mesh,
        in_specs=placed,
        out_specs=(
            P("dp", "ctx", None),
            P("dp", "ctx", None),
            P("dp", "ctx", None),
            P("dp", "ctx", None),
            P("ctx", None),
        ),
        check_vma=False,
    )
```

```python
import functools

import jax
import jax.numpy as jnp
from jax import lax
from jax.experimental import pallas as pl
from jax.experimental.pallas import tpu as pltpu
from jax.sharding import PartitionSpec as P

HD = 64
BLK = 128
GW = 2 * HD
NG = 4
WIN = 3 * BLK
BF = jnp.bfloat16
F32 = jnp.float32
MESH = pl.DeviceIdType.MESH
NEG = -1e30


def nn(a, b):
    return lax.dot_general(a, b, (((1,), (0,)), ((), ())), preferred_element_type=F32)


def nt(a, b):
    return lax.dot_general(a, b, (((1,), (1,)), ((), ())), preferred_element_type=F32)


def block_diag(rows):
    lane = lax.broadcasted_iota(jnp.int32, rows.shape, 1)
    zero = jnp.zeros_like(rows)
    return jnp.concatenate([jnp.where(lane < HD, rows, zero), jnp.where(lane < HD, zero, rows)], axis=0)


def diagonal(both):
    return jnp.concatenate([both[:HD, :BLK], both[HD:, BLK:]], axis=0)


def kernel(
    dims, wscale,
    q_hbm, k_hbm, v_hbm, g_hbm, w_hbm, mask_hbm,
    out_s, dq_s, dk_s, dv_s, dw_s,
    mask, q_s, k_ext, v_ext, g_s, w_s, k_t, v_t, da_t, qbd, abd, p_t, at, dw_own,
    csend, crecv, xsend, xrecv, zsend, zrecv, ysend, yrecv,
    dk_acc, dv_acc, gsend, grecv, dq_t,
    lsem, h_s, h_r, c_s, c_r, x_s, x_r, z_s, z_r, y_s, y_r, g_ss, g_rs,
):
    NY, ZH, ZL, NX = dims
    NZ = ZL * ZH
    CTX = ZL * NX * 2
    dp = lax.axis_index("dp")
    ctx = lax.axis_index("ctx")
    y, zh = dp // ZH, dp % ZH
    zl, x, core = ctx // (NX * 2), (ctx // 2) % NX, ctx % 2
    z = zh * ZL + zl

    def ident(y_, z_, x_, c_):
        return (y_ * ZH + z_ // ZL, (z_ % ZL) * (NX * 2) + x_ * 2 + c_)

    right = (dp, (ctx + 1) % CTX)
    left = (dp, (ctx + CTX - 1) % CTX)
    mate = (dp, ctx + 1 - 2 * core)
    x_peer = [ident(y, z, (x + d) % NX, core) for d in range(1, NX)]
    y_peer = [ident((y + d) % NY, z, x, core) for d in range(1, NY)]
    z_peer = [ident(y, (z + d) % NZ, x, core) for d in range(1, NZ)]

    def remote(src, dst, ssem, rsem, dev):
        return pltpu.make_async_remote_copy(
            src_ref=src, dst_ref=dst, send_sem=ssem, recv_sem=rsem, device_id=dev, device_id_type=MESH
        )

    barrier = pltpu.get_barrier_semaphore()
    peers = [right, left] + x_peer + y_peer + z_peer
    for dev in peers:
        pl.semaphore_signal(barrier, inc=1, device_id=dev, device_id_type=MESH)

    own = pl.ds(BLK, 2 * BLK)
    load_g = pltpu.make_async_copy(g_hbm, g_s, lsem.at[0])
    load_w = pltpu.make_async_copy(w_hbm, w_s, lsem.at[1])
    load_q = pltpu.make_async_copy(q_hbm, q_s, lsem.at[2])
    load_k = pltpu.make_async_copy(k_hbm, k_ext.at[own], lsem.at[3])
    load_v = pltpu.make_async_copy(v_hbm, v_ext.at[own], lsem.at[4])
    load_m = pltpu.make_async_copy(mask_hbm, mask, lsem.at[5])
    loads = [load_m, load_g, load_w, load_q, load_k, load_v]
    for copy in loads:
        copy.start()

    pl.semaphore_wait(barrier, len(peers))

    first, last = pl.ds(0, BLK), pl.ds(BLK, BLK)
    low, high = pl.ds(0, BLK), pl.ds(3 * BLK, BLK)

    def halo_copies(g):
        c = pl.ds(g * GW, GW)
        return [
            remote(k_hbm.at[last, c], k_ext.at[low, c], h_s.at[g, 0], h_r.at[g, 0], right),
            remote(k_hbm.at[first, c], k_ext.at[high, c], h_s.at[g, 1], h_r.at[g, 1], left),
            remote(v_hbm.at[last, c], v_ext.at[low, c], h_s.at[g, 2], h_r.at[g, 2], right),
            remote(v_hbm.at[first, c], v_ext.at[high, c], h_s.at[g, 3], h_r.at[g, 3], left),
        ]

    for g in range(NG):
        for copy in halo_copies(g):
            copy.start()

    def cols(g):
        return slice(g * GW, (g + 1) * GW)

    load_q.wait()
    for b in range(2):
        for g in range(NG):
            scaled = q_s[b * BLK:(b + 1) * BLK, cols(g)] * jnp.asarray(HD ** -0.5, BF)
            qbd[b, g] = block_diag(scaled)
    load_v.wait()
    v_t[:, BLK:3 * BLK] = v_ext[BLK:3 * BLK, :].T
    load_k.wait()
    k_t[:, BLK:3 * BLK] = k_ext[BLK:3 * BLK, :].T
    load_g.wait()
    load_w.wait()
    da = nt(g_s[...], w_s[...]).astype(BF)
    for b in range(2):
        for g in range(NG):
            abd[b, g] = block_diag(da[b * BLK:(b + 1) * BLK, cols(g)])
    da_t[...] = nt(w_s[...], g_s[...]).astype(BF)

    load_m.wait()
    bias = []
    for b in range(2):
        row = ctx * 2 + b
        bias.append([jnp.where(mask[c, 0, row] == 1, 0.0, NEG).astype(F32) for c in (0, 2)])

    def window(b):
        return slice(b * BLK, b * BLK + WIN)

    def forward(g):
        for copy in halo_copies(g):
            copy.wait_recv()
        v_t[cols(g), :BLK] = v_ext[:BLK, cols(g)].T
        v_t[cols(g), 3 * BLK:] = v_ext[3 * BLK:, cols(g)].T
        parts = []
        for b in range(2):
            s = nt(k_ext[window(b), cols(g)], qbd[b, g])
            lo, mid, hi = s[:BLK], s[BLK:2 * BLK], s[2 * BLK:]
            b_lo, b_hi = bias[b]
            top = jnp.maximum(
                jnp.max(mid, axis=0, keepdims=True),
                jnp.maximum(jnp.max(lo, axis=0, keepdims=True) + b_lo, jnp.max(hi, axis=0, keepdims=True) + b_hi),
            )
            e_lo = jnp.exp(lo - (top - b_lo))
            e_mid = jnp.exp(mid - top)
            e_hi = jnp.exp(hi - (top - b_hi))
            total = jnp.sum(e_lo + e_mid + e_hi, axis=0, keepdims=True)
            inv = 1.0 / total
            p = jnp.concatenate([(e_lo * inv).astype(BF), (e_mid * inv).astype(BF), (e_hi * inv).astype(BF)], axis=0)
            p_t[b, g] = p
            parts.append(diagonal(nn(v_t[cols(g), window(b)], p)).astype(BF))
        rows = jnp.concatenate(parts, axis=1)
        at[g] = rows.reshape(4, 2, 16, 2 * BLK)

    def core_copy(g):
        return remote(csend.at[g], crecv.at[g], c_s.at[g], c_r.at[g], mate)

    def x_copy(g, d):
        return remote(xsend.at[g, (x + d) % NX], xrecv.at[g, d - 1], x_s.at[g, d - 1], x_r.at[g, d - 1], x_peer[d - 1])

    def z_copy(g, side):
        t = side * ZL + g
        slot = (t + NZ - z) % NZ - 1
        return remote(zsend.at[g], zrecv.at[slot], z_s.at[g, side], z_r.at[slot], ident(y, t, x, core))

    def z_arrival(slot):
        return remote(zsend.at[0], zrecv.at[slot], z_s.at[0, 0], z_r.at[slot], z_peer[slot])

    def y_copy(d):
        return remote(ysend, yrecv.at[d - 1], y_s.at[d - 1], y_r.at[d - 1], y_peer[d - 1])

    def weight_part(g):
        mine = at[g, :, core].reshape(64, 2 * BLK)
        other = at[g, :, 1 - core].reshape(64, 2 * BLK)
        part = nn(jnp.concatenate([mine, other], axis=0), g_s[...])
        csend[g] = part[64:].astype(BF)
        dw_own[g] = part[:64]
        core_copy(g).start()

    def core_sum(g):
        core_copy(g).wait_recv()
        total = dw_own[g] + crecv[g].astype(F32)
        xsend[g] = total.astype(BF).reshape(4, 16, 1024)
        for d in range(1, NX):
            x_copy(g, d).start()

    def z_each(g, act):
        for side in range(ZH):
            @pl.when(z != side * ZL + g)
            def _():
                act(z_copy(g, side))

    def x_sum(g):
        total = xsend[g, x].astype(F32)
        for d in range(1, NX):
            x_copy(g, d).wait_recv()
            total += xrecv[g, d - 1].astype(F32)
        zsend[g] = total.astype(BF)
        if g < ZL:
            z_each(g, lambda copy: copy.start())

    def z_sum():
        total = zsend[z % ZL].astype(F32)
        for slot in range(NZ - 1):
            z_arrival(slot).wait_recv()
            total += zrecv[slot].astype(F32)
        ysend[...] = total.astype(BF)
        for d in range(1, NY):
            y_copy(d).start()

    def y_sum():
        total = ysend[...].astype(F32)
        for d in range(1, NY):
            y_copy(d).wait_recv()
            total += yrecv[d - 1].astype(F32)
        dw_s[...] = total * wscale

    def grad_copy(side, g):
        return remote(gsend.at[side, g], grecv.at[side, g], g_ss.at[side, g], g_rs.at[side, g], right if side else left)

    def backward(g):
        tok = [slice(0, BLK), slice(BLK, 2 * BLK)]
        k_win, v_win = [], []
        rows = at[g].reshape(GW, 2 * BLK)
        q_parts = []
        for b in range(2):
            prod = rows[:, tok[b]].astype(F32) * da_t[cols(g), tok[b]].astype(F32)
            delta = jnp.concatenate(
                [jnp.sum(prod[:HD], axis=0, keepdims=True), jnp.sum(prod[HD:], axis=0, keepdims=True)], axis=1
            )
            dp_t = nt(v_ext[window(b), cols(g)], abd[b, g])
            p = p_t[b, g]
            ds = (p.astype(F32) * (dp_t - delta)).astype(BF)
            v_win.append(nn(p, abd[b, g]))
            k_win.append(nn(ds, qbd[b, g]))
            q_parts.append((diagonal(nn(k_t[cols(g), window(b)], ds)) * (HD ** -0.5)).astype(BF))
        for n, win in enumerate((k_win, v_win)):
            gsend[0, g, n] = win[0][:BLK].astype(BF)
            gsend[1, g, n] = win[1][2 * BLK:].astype(BF)
        grad_copy(0, g).start()
        grad_copy(1, g).start()
        dk_acc[g] = k_win[0][BLK:] + k_win[1][:2 * BLK]
        dv_acc[g] = v_win[0][BLK:] + v_win[1][:2 * BLK]
        dq_t[cols(g), :] = jnp.concatenate(q_parts, axis=1)

    for g in range(NG):
        forward(g)
        weight_part(g)
        if g >= 1:
            core_sum(g - 1)
    k_t[:, :BLK] = k_ext[:BLK, :].T
    k_t[:, 3 * BLK:] = k_ext[3 * BLK:, :].T
    backward(0)
    core_sum(NG - 1)
    x_sum(0)
    backward(1)
    x_sum(1)
    backward(2)
    x_sum(2)
    backward(3)
    dq_s[...] = dq_t[...].T
    x_sum(3)
    attn = at[...].reshape(NG * GW, 2 * BLK).T
    out_s[...] = nn(attn, w_s[...]).astype(BF)
    for g in range(NG):
        grad_copy(0, g).wait_recv()
        grad_copy(1, g).wait_recv()
        for n, (acc, dst) in enumerate(((dk_acc, dk_s), (dv_acc, dv_s))):
            dst[:BLK, cols(g)] = (acc[g, :BLK] + grecv[1, g, n].astype(F32)).astype(BF)
            dst[BLK:, cols(g)] = (acc[g, BLK:] + grecv[0, g, n].astype(F32)).astype(BF)
    z_sum()

    for g in range(NG):
        for copy in halo_copies(g):
            copy.wait_send()
        core_copy(g).wait_send()
        for d in range(1, NX):
            x_copy(g, d).wait_send()
        if g < ZL:
            z_each(g, lambda copy: copy.wait_send())
        grad_copy(0, g).wait_send()
        grad_copy(1, g).wait_send()
    y_sum()
    for d in range(1, NY):
        y_copy(d).wait_send()


def store_kernel(*refs):
    srcs, dsts, sem = refs[:5], refs[5:10], refs[10]
    copies = [pltpu.make_async_copy(src, dst, sem.at[n]) for n, (src, dst) in enumerate(zip(srcs, dsts))]
    for copy in copies:
        copy.start()
    for copy in copies:
        copy.wait()


def pinned(array, space):
    return pltpu.with_memory_space_constraint(array, space)


def body(dims, wscale, queries, keys, values, out_grad, w_out, block_mask):
    NY, ZH, ZL, NX = dims
    NZ = ZL * ZH
    tok, feat = queries.shape[1:]
    width = w_out.shape[1]
    free = pl.BlockSpec(memory_space=pl.ANY)
    vm = pltpu.VMEM
    dma = pltpu.SemaphoreType.DMA
    nx, ny, nz = max(NX - 1, 1), max(NY - 1, 1), max(NZ - 1, 1)
    shapes = (
        jax.ShapeDtypeStruct((tok, width), BF),
        jax.ShapeDtypeStruct((tok, feat), BF),
        jax.ShapeDtypeStruct((tok, feat), BF),
        jax.ShapeDtypeStruct((tok, feat), BF),
        jax.ShapeDtypeStruct((16, width), F32),
    )
    mask = jnp.transpose(block_mask, (2, 0, 1))
    arrays = [pinned(a, pltpu.HBM) for a in (queries[0], keys[0], values[0], out_grad[0], w_out, mask)]
    outs = pl.pallas_call(
        functools.partial(kernel, dims, wscale),
        out_shape=tuple(vm(a.shape, a.dtype) for a in shapes),
        in_specs=[free] * 6,
        out_specs=[pl.BlockSpec(memory_space=vm)] * 5,
        scratch_shapes=[
            pltpu.SMEM((block_mask.shape[2], 1, block_mask.shape[1]), jnp.int32),
            vm((tok, feat), BF),
            vm((4 * BLK, feat), BF),
            vm((4 * BLK, feat), BF),
            vm((tok, width), BF),
            vm((feat, width), BF),
            vm((feat, 4 * BLK), BF),
            vm((feat, 4 * BLK), BF),
            vm((feat, tok), BF),
            vm((2, NG, 2 * BLK, GW), BF),
            vm((2, NG, 2 * BLK, GW), BF),
            vm((2, NG, WIN, 2 * BLK), BF),
            vm((NG, 4, 2, 16, tok), BF),
            vm((NG, 64, width), F32),
            vm((NG, 64, width), BF),
            vm((NG, 64, width), BF),
            vm((NG, 4, 16, width), BF),
            vm((NG, nx, 16, width), BF),
            vm((NG, 16, width), BF),
            vm((nz, 16, width), BF),
            vm((16, width), BF),
            vm((ny, 16, width), BF),
            vm((NG, tok, GW), F32),
            vm((NG, tok, GW), F32),
            vm((2, NG, 2, BLK, GW), BF),
            vm((2, NG, 2, BLK, GW), BF),
            vm((feat, tok), BF),
            dma((6,)),
            dma((NG, 4)), dma((NG, 4)),
            dma((NG,)), dma((NG,)),
            dma((NG, nx)), dma((NG, nx)),
            dma((NG, 2)), dma((nz,)),
            dma((ny,)), dma((ny,)),
            dma((2, NG)), dma((2, NG)),
        ],
        compiler_params=pltpu.CompilerParams(
            collective_id=0, has_side_effects=True, vmem_limit_bytes=40 * 1024 * 1024
        ),
    )(*arrays)
    outs = pl.pallas_call(
        store_kernel,
        out_shape=shapes,
        in_specs=[pl.BlockSpec(memory_space=vm)] * 5,
        out_specs=[free] * 5,
        scratch_shapes=[dma((5,))],
    )(*[pinned(a, vm) for a in outs])
    return (outs[0][None], outs[1][None], outs[2][None], outs[3][None], outs[4])


def solution(mesh, dims=(8, 2, 4, 4)):
    tokens = mesh.shape["dp"] * mesh.shape["ctx"] * 256
    placed = (
        P("dp", "ctx", None),
        P("dp", "ctx", None),
        P("dp", "ctx", None),
        P("dp", "ctx", None),
        P(),
        P("dp", None, None),
    )
    return jax.shard_map(
        functools.partial(body, dims, tokens ** -0.5),
        mesh=mesh,
        in_specs=placed,
        out_specs=(
            P("dp", "ctx", None),
            P("dp", "ctx", None),
            P("dp", "ctx", None),
            P("dp", "ctx", None),
            P("ctx", None),
        ),
        check_vma=False,
    )
```

```python
import functools

import jax
import jax.numpy as jnp
from jax import lax
from jax.experimental import pallas as pl
from jax.experimental.pallas import tpu as pltpu
from jax.sharding import PartitionSpec as P

HD = 64
BLK = 128
GW = 2 * HD
NG = 4
WIN = 3 * BLK
BF = jnp.bfloat16
F32 = jnp.float32
MESH = pl.DeviceIdType.MESH
NEG = -1e30


def nn(a, b):
    return lax.dot_general(a, b, (((1,), (0,)), ((), ())), preferred_element_type=F32)


def nt(a, b):
    return lax.dot_general(a, b, (((1,), (1,)), ((), ())), preferred_element_type=F32)


def block_diag(rows):
    lane = lax.broadcasted_iota(jnp.int32, rows.shape, 1)
    zero = jnp.zeros_like(rows)
    return jnp.concatenate([jnp.where(lane < HD, rows, zero), jnp.where(lane < HD, zero, rows)], axis=0)


def diagonal(both):
    return jnp.concatenate([both[:HD, :BLK], both[HD:, BLK:]], axis=0)


def kernel(
    dims, wscale,
    q_hbm, k_hbm, v_hbm, g_hbm, w_hbm, mask_hbm,
    out_s, dq_s, dk_s, dv_s, dw_s,
    mask, q_s, k_ext, v_ext, g_s, w_s, k_t, v_t, da_t, qbd, abd, e_own, e_halo, o_own, stats, at, dw_own,
    csend, crecv, xsend, xrecv, zsend, zrecv, ysend, yrecv,
    dk_acc, dv_acc, gsend, grecv, dq_t,
    lsem, h_s, h_r, c_s, c_r, x_s, x_r, z_s, z_r, y_s, y_r, g_ss, g_rs,
):
    NY, ZH, ZL, NX = dims
    NZ = ZL * ZH
    CTX = ZL * NX * 2
    dp = lax.axis_index("dp")
    ctx = lax.axis_index("ctx")
    y, zh = dp // ZH, dp % ZH
    zl, x, core = ctx // (NX * 2), (ctx // 2) % NX, ctx % 2
    z = zh * ZL + zl

    def ident(y_, z_, x_, c_):
        return (y_ * ZH + z_ // ZL, (z_ % ZL) * (NX * 2) + x_ * 2 + c_)

    right = (dp, (ctx + 1) % CTX)
    left = (dp, (ctx + CTX - 1) % CTX)
    mate = (dp, ctx + 1 - 2 * core)
    x_peer = [ident(y, z, (x + d) % NX, core) for d in range(1, NX)]
    y_peer = [ident((y + d) % NY, z, x, core) for d in range(1, NY)]
    z_peer = [ident(y, (z + d) % NZ, x, core) for d in range(1, NZ)]

    def remote(src, dst, ssem, rsem, dev):
        return pltpu.make_async_remote_copy(
            src_ref=src, dst_ref=dst, send_sem=ssem, recv_sem=rsem, device_id=dev, device_id_type=MESH
        )

    own = pl.ds(BLK, 2 * BLK)
    load_g = pltpu.make_async_copy(g_hbm, g_s, lsem.at[0])
    load_w = pltpu.make_async_copy(w_hbm, w_s, lsem.at[1])
    load_q = pltpu.make_async_copy(q_hbm, q_s, lsem.at[2])
    load_k = pltpu.make_async_copy(k_hbm, k_ext.at[own], lsem.at[3])
    load_v = pltpu.make_async_copy(v_hbm, v_ext.at[own], lsem.at[4])
    load_m = pltpu.make_async_copy(mask_hbm, mask, lsem.at[5])
    loads = [load_q, load_m, load_v, load_k, load_g, load_w]
    for copy in loads:
        copy.start()

    barrier = pltpu.get_barrier_semaphore()
    peers = [right, left] + x_peer + y_peer + z_peer
    for dev in peers:
        pl.semaphore_signal(barrier, inc=1, device_id=dev, device_id_type=MESH)

    pl.semaphore_wait(barrier, len(peers))

    first, last = pl.ds(0, BLK), pl.ds(BLK, BLK)
    low, high = pl.ds(0, BLK), pl.ds(3 * BLK, BLK)

    def halo_copy(n, g):
        c = pl.ds(g * GW, GW)
        src, dst = (k_hbm, k_ext) if n < 2 else (v_hbm, v_ext)
        if n % 2:
            return remote(src.at[first, c], dst.at[high, c], h_s.at[g, n], h_r.at[g, n], left)
        return remote(src.at[last, c], dst.at[low, c], h_s.at[g, n], h_r.at[g, n], right)

    def halo_send(g):
        for n in range(4):
            halo_copy(n, g).start()

    halo_send(0)

    def cols(g):
        return slice(g * GW, (g + 1) * GW)

    def rows_of(stat):
        return jnp.concatenate(
            [jnp.broadcast_to(stat[:, :BLK], (HD, BLK)), jnp.broadcast_to(stat[:, BLK:], (HD, BLK))], axis=0
        )

    load_q.wait()
    for b in range(2):
        for g in range(NG):
            scaled = q_s[b * BLK:(b + 1) * BLK, cols(g)] * jnp.asarray(HD ** -0.5, BF)
            qbd[b, g] = block_diag(scaled)
    load_m.wait()
    bias = []
    for b in range(2):
        row = ctx * 2 + b
        bias.append([jnp.where(mask[c, 0, row] == 1, 0.0, NEG).astype(F32) for c in (0, 2)])
    load_v.wait()
    v_t[:, BLK:3 * BLK] = v_ext[BLK:3 * BLK, :].T
    load_k.wait()

    def own_part(g):
        for b in range(2):
            s = nt(k_ext[BLK:3 * BLK, cols(g)], qbd[b, g])
            mid, other = s[b * BLK:(b + 1) * BLK], s[(1 - b) * BLK:(2 - b) * BLK]
            b_other = bias[b][1 - b]
            top = jnp.maximum(jnp.max(mid, axis=0, keepdims=True), jnp.max(other, axis=0, keepdims=True) + b_other)
            e_mid = jnp.exp(mid - top)
            e_other = jnp.exp(other - (top - b_other))
            total = jnp.sum(e_mid + e_other, axis=0, keepdims=True)
            pair = (e_mid, e_other) if b == 0 else (e_other, e_mid)
            e = jnp.concatenate(pair, axis=0).astype(BF)
            e_own[b, g] = e
            o_own[b, g] = diagonal(nn(v_t[cols(g), BLK:3 * BLK], e))
            stats[b, g, 0:1] = top
            stats[b, g, 1:2] = total

    def window(b):
        return slice(b * BLK, b * BLK + WIN)

    def halo_at(b):
        return slice(3 * b * BLK, 3 * b * BLK + BLK)

    def forward(g):
        parts = []
        for n in range(2):
            halo_copy(n, g).wait_recv()
        exps = []
        for b in range(2):
            s = nt(k_ext[halo_at(b), cols(g)], qbd[b, g])
            b_halo = bias[b][b]
            top_own = stats[b, g, 0:1]
            top = jnp.maximum(top_own, jnp.max(s, axis=0, keepdims=True) + b_halo)
            e = jnp.exp(s - (top - b_halo))
            shrink = jnp.exp(top_own - top)
            inv = 1.0 / (stats[b, g, 1:2] * shrink + jnp.sum(e, axis=0, keepdims=True))
            e = e.astype(BF)
            e_halo[b, g] = e
            stats[b, g, 2:3] = shrink * inv
            stats[b, g, 3:4] = inv
            exps.append((e, shrink * inv, inv))
        for n in range(2, 4):
            halo_copy(n, g).wait_recv()
        for b in range(2):
            e, f_own, f_halo = exps[b]
            o_halo = diagonal(nn(v_ext[halo_at(b), cols(g)].T, e))
            parts.append((o_own[b, g] * rows_of(f_own) + o_halo * rows_of(f_halo)).astype(BF))
        rows = jnp.concatenate(parts, axis=1)
        at[g] = rows.reshape(4, 2, 16, 2 * BLK)

    def core_copy(g):
        return remote(csend.at[g], crecv.at[g], c_s.at[g], c_r.at[g], mate)

    def x_copy(g, d):
        return remote(xsend.at[g, (x + d) % NX], xrecv.at[g, d - 1], x_s.at[g, d - 1], x_r.at[g, d - 1], x_peer[d - 1])

    def z_copy(g, side):
        t = side * ZL + g
        slot = (t + NZ - z) % NZ - 1
        return remote(zsend.at[g], zrecv.at[slot], z_s.at[g, side], z_r.at[slot], ident(y, t, x, core))

    def z_arrival(slot):
        return remote(zsend.at[0], zrecv.at[slot], z_s.at[0, 0], z_r.at[slot], z_peer[slot])

    def z_each(g, act):
        for side in range(ZH):
            @pl.when(z != side * ZL + g)
            def _():
                act(z_copy(g, side))

    def y_copy(j):
        slot = (j + NY - y) % NY - 1
        return remote(ysend, yrecv.at[slot], y_s.at[slot], y_r.at[slot], ident(j, z, x, core))

    def y_arrival(d):
        return remote(ysend, yrecv.at[d - 1], y_s.at[d - 1], y_r.at[d - 1], y_peer[d - 1])

    def y_each(act):
        for j in range(NY):
            @pl.when(y != j)
            def _():
                act(y_copy(j))

    def weight_part(g):
        mine = at[g, :, core].reshape(64, 2 * BLK)
        other = at[g, :, 1 - core].reshape(64, 2 * BLK)
        part = nn(jnp.concatenate([mine, other], axis=0), g_s[...])
        csend[g] = part[64:].astype(BF)
        dw_own[g] = part[:64]
        core_copy(g).start()

    def core_sum(g):
        core_copy(g).wait_recv()
        total = dw_own[g] + crecv[g].astype(F32)
        xsend[g] = total.astype(BF).reshape(4, 16, 1024)
        for d in sorted(range(1, NX), key=lambda d: -min(d, NX - d)):
            x_copy(g, d).start()

    def x_sum(g):
        total = xsend[g, x].astype(F32)
        for d in range(1, NX):
            x_copy(g, d).wait_recv()
            total += xrecv[g, d - 1].astype(F32)
        zsend[g] = total.astype(BF)
        z_each(g, lambda copy: copy.start())

    def z_sum(g):
        @pl.when(z % ZL == g)
        def _():
            total = zsend[g].astype(F32)
            for slot in range(NZ - 1):
                z_arrival(slot).wait_recv()
                total += zrecv[slot].astype(F32)
            ysend[...] = total.astype(BF)
            y_each(lambda copy: copy.start())

    def y_sum():
        total = ysend[...].astype(F32)
        for d in range(1, NY):
            y_arrival(d).wait_recv()
            total += yrecv[d - 1].astype(F32)
        dw_s[...] = total * wscale

    def grad_copy(side, g):
        return remote(gsend.at[side, g], grecv.at[side, g], g_ss.at[side, g], g_rs.at[side, g], right if side else left)

    def backward(g):
        tok = [slice(0, BLK), slice(BLK, 2 * BLK)]
        k_win, v_win = [], []
        rows = at[g].reshape(GW, 2 * BLK)
        q_parts = []
        for b in range(2):
            prod = rows[:, tok[b]].astype(F32) * da_t[cols(g), tok[b]].astype(F32)
            delta = jnp.concatenate(
                [jnp.sum(prod[:HD], axis=0, keepdims=True), jnp.sum(prod[HD:], axis=0, keepdims=True)], axis=1
            )
            dp_t = nt(v_ext[window(b), cols(g)], abd[b, g])
            p_own = e_own[b, g].astype(F32) * stats[b, g, 2:3]
            p_halo = e_halo[b, g].astype(F32) * stats[b, g, 3:4]
            p_all = jnp.concatenate((p_halo, p_own) if b == 0 else (p_own, p_halo), axis=0)
            p = p_all.astype(BF)
            ds = (p_all * (dp_t - delta)).astype(BF)
            v_win.append(nn(p, abd[b, g]))
            k_win.append(nn(ds, qbd[b, g]))
            q_parts.append((diagonal(nn(k_t[cols(g), window(b)], ds)) * (HD ** -0.5)).astype(BF))
        for n, win in enumerate((k_win, v_win)):
            gsend[0, g, n] = win[0][:BLK].astype(BF)
            gsend[1, g, n] = win[1][2 * BLK:].astype(BF)
        grad_copy(0, g).start()
        grad_copy(1, g).start()
        dk_acc[g] = k_win[0][BLK:] + k_win[1][:2 * BLK]
        dv_acc[g] = v_win[0][BLK:] + v_win[1][:2 * BLK]
        dq_t[cols(g), :] = jnp.concatenate(q_parts, axis=1)

    own_part(0)
    halo_send(1)
    own_part(1)
    halo_send(2)
    halo_send(3)
    own_part(2)
    load_g.wait()
    forward(0)
    weight_part(0)
    own_part(3)
    forward(1)
    weight_part(1)
    core_sum(0)
    forward(2)
    weight_part(2)
    core_sum(1)
    forward(3)
    weight_part(3)
    core_sum(2)
    load_w.wait()
    da = nt(g_s[...], w_s[...]).astype(BF)
    for b in range(2):
        for g in range(NG):
            abd[b, g] = block_diag(da[b * BLK:(b + 1) * BLK, cols(g)])
    core_sum(3)
    da_t[...] = nt(w_s[...], g_s[...]).astype(BF)
    k_t[...] = k_ext[...].T
    x_sum(0)
    backward(0)
    x_sum(1)
    backward(1)
    x_sum(2)
    x_sum(3)
    backward(2)
    z_sum(0)
    backward(3)
    z_sum(1)
    attn = at[...].reshape(NG * GW, 2 * BLK).T
    out_s[...] = nn(attn, w_s[...]).astype(BF)
    z_sum(2)
    dq_s[...] = dq_t[...].T
    z_sum(3)

    for g in range(NG):
        grad_copy(0, g).wait_recv()
        grad_copy(1, g).wait_recv()
        for n, (acc, dst) in enumerate(((dk_acc, dk_s), (dv_acc, dv_s))):
            dst[:BLK, cols(g)] = (acc[g, :BLK] + grecv[1, g, n].astype(F32)).astype(BF)
            dst[BLK:, cols(g)] = (acc[g, BLK:] + grecv[0, g, n].astype(F32)).astype(BF)
    for g in range(NG):
        for n in range(4):
            halo_copy(n, g).wait_send()
        core_copy(g).wait_send()
        for d in range(1, NX):
            x_copy(g, d).wait_send()
        z_each(g, lambda copy: copy.wait_send())
        grad_copy(0, g).wait_send()
        grad_copy(1, g).wait_send()
    y_sum()
    y_each(lambda copy: copy.wait_send())


def store_kernel(*refs):
    srcs, dsts, sem = refs[:5], refs[5:10], refs[10]
    copies = [pltpu.make_async_copy(src, dst, sem.at[n]) for n, (src, dst) in enumerate(zip(srcs, dsts))]
    for copy in copies:
        copy.start()
    for copy in copies:
        copy.wait()


def pinned(array, space):
    return pltpu.with_memory_space_constraint(array, space)


def body(dims, wscale, queries, keys, values, out_grad, w_out, block_mask):
    NY, ZH, ZL, NX = dims
    NZ = ZL * ZH
    tok, feat = queries.shape[1:]
    width = w_out.shape[1]
    free = pl.BlockSpec(memory_space=pl.ANY)
    vm = pltpu.VMEM
    dma = pltpu.SemaphoreType.DMA
    nx, ny, nz = max(NX - 1, 1), max(NY - 1, 1), max(NZ - 1, 1)
    shapes = (
        jax.ShapeDtypeStruct((tok, width), BF),
        jax.ShapeDtypeStruct((tok, feat), BF),
        jax.ShapeDtypeStruct((tok, feat), BF),
        jax.ShapeDtypeStruct((tok, feat), BF),
        jax.ShapeDtypeStruct((16, width), F32),
    )
    mask = jnp.transpose(block_mask, (2, 0, 1))
    arrays = [pinned(a, pltpu.HBM) for a in (queries[0], keys[0], values[0], out_grad[0], w_out, mask)]
    outs = pl.pallas_call(
        functools.partial(kernel, dims, wscale),
        out_shape=tuple(vm(a.shape, a.dtype) for a in shapes),
        in_specs=[free] * 6,
        out_specs=[pl.BlockSpec(memory_space=vm)] * 5,
        scratch_shapes=[
            pltpu.SMEM((block_mask.shape[2], 1, block_mask.shape[1]), jnp.int32),
            vm((tok, feat), BF),
            vm((4 * BLK, feat), BF),
            vm((4 * BLK, feat), BF),
            vm((tok, width), BF),
            vm((feat, width), BF),
            vm((feat, 4 * BLK), BF),
            vm((feat, 4 * BLK), BF),
            vm((feat, tok), BF),
            vm((2, NG, 2 * BLK, GW), BF),
            vm((2, NG, 2 * BLK, GW), BF),
            vm((2, NG, 2 * BLK, 2 * BLK), BF),
            vm((2, NG, BLK, 2 * BLK), BF),
            vm((2, NG, GW, BLK), F32),
            vm((2, NG, 8, 2 * BLK), F32),
            vm((NG, 4, 2, 16, tok), BF),
            vm((NG, 64, width), F32),
            vm((NG, 64, width), BF),
            vm((NG, 64, width), BF),
            vm((NG, 4, 16, width), BF),
            vm((NG, nx, 16, width), BF),
            vm((NG, 16, width), BF),
            vm((nz, 16, width), BF),
            vm((16, width), BF),
            vm((ny, 16, width), BF),
            vm((NG, tok, GW), F32),
            vm((NG, tok, GW), F32),
            vm((2, NG, 2, BLK, GW), BF),
            vm((2, NG, 2, BLK, GW), BF),
            vm((feat, tok), BF),
            dma((6,)),
            dma((NG, 4)), dma((NG, 4)),
            dma((NG,)), dma((NG,)),
            dma((NG, nx)), dma((NG, nx)),
            dma((NG, 2)), dma((nz,)),
            dma((ny,)), dma((ny,)),
            dma((2, NG)), dma((2, NG)),
        ],
        compiler_params=pltpu.CompilerParams(
            collective_id=0, has_side_effects=True, vmem_limit_bytes=40 * 1024 * 1024
        ),
    )(*arrays)
    outs = pl.pallas_call(
        store_kernel,
        out_shape=shapes,
        in_specs=[pl.BlockSpec(memory_space=vm)] * 5,
        out_specs=[free] * 5,
        scratch_shapes=[dma((5,))],
    )(*[pinned(a, vm) for a in outs])
    return (outs[0][None], outs[1][None], outs[2][None], outs[3][None], outs[4])


def solution(mesh, dims=(8, 2, 4, 4)):
    tokens = mesh.shape["dp"] * mesh.shape["ctx"] * 256
    placed = (
        P("dp", "ctx", None),
        P("dp", "ctx", None),
        P("dp", "ctx", None),
        P("dp", "ctx", None),
        P(),
        P("dp", None, None),
    )
    return jax.shard_map(
        functools.partial(body, dims, tokens ** -0.5),
        mesh=mesh,
        in_specs=placed,
        out_specs=(
            P("dp", "ctx", None),
            P("dp", "ctx", None),
            P("dp", "ctx", None),
            P("dp", "ctx", None),
            P("ctx", None),
        ),
        check_vma=False,
    )
```

```python
import functools

import jax
import jax.numpy as jnp
from jax import lax
from jax.experimental import pallas as pl
from jax.experimental.pallas import tpu as pltpu
from jax.sharding import PartitionSpec as P

HD = 64
BLK = 128
GW = 2 * HD
NG = 4
WIN = 3 * BLK
BF = jnp.bfloat16
F32 = jnp.float32
MESH = pl.DeviceIdType.MESH
NEG = -1e30


def nn(a, b):
    return lax.dot_general(a, b, (((1,), (0,)), ((), ())), preferred_element_type=F32)


def nt(a, b):
    return lax.dot_general(a, b, (((1,), (1,)), ((), ())), preferred_element_type=F32)


def block_diag(rows):
    lane = lax.broadcasted_iota(jnp.int32, rows.shape, 1)
    zero = jnp.zeros_like(rows)
    return jnp.concatenate([jnp.where(lane < HD, rows, zero), jnp.where(lane < HD, zero, rows)], axis=0)


def diagonal(both):
    return jnp.concatenate([both[:HD, :BLK], both[HD:, BLK:]], axis=0)


def kernel(
    dims, wscale,
    q_hbm, k_hbm, v_hbm, g_hbm, w_hbm, mask_hbm,
    out_s, dq_s, dk_s, dv_s, dw_s,
    mask, q_s, k_ext, v_ext, g_s, w_s, k_t, v_t, da_t, qbd, abd, e_own, e_halo, o_own, stats, at, dw_own,
    csend, crecv, xsend, xrecv, zsend, zrecv, ysend, yrecv,
    dk_acc, dv_acc, gsend, grecv, dq_t,
    lsem, h_s, h_r, c_s, c_r, x_s, x_r, z_s, z_r, y_s, y_r, g_ss, g_rs,
):
    NY, ZH, ZL, NX = dims
    NZ = ZL * ZH
    CTX = ZL * NX * 2
    dp = lax.axis_index("dp")
    ctx = lax.axis_index("ctx")
    y, zh = dp // ZH, dp % ZH
    zl, x, core = ctx // (NX * 2), (ctx // 2) % NX, ctx % 2
    z = zh * ZL + zl

    def ident(y_, z_, x_, c_):
        return (y_ * ZH + z_ // ZL, (z_ % ZL) * (NX * 2) + x_ * 2 + c_)

    right = (dp, (ctx + 1) % CTX)
    left = (dp, (ctx + CTX - 1) % CTX)
    mate = (dp, ctx + 1 - 2 * core)
    x_peer = [ident(y, z, (x + d) % NX, core) for d in range(1, NX)]
    y_peer = [ident((y + d) % NY, z, x, core) for d in range(1, NY)]
    z_peer = [ident(y, (z + d) % NZ, x, core) for d in range(1, NZ)]

    def remote(src, dst, ssem, rsem, dev):
        return pltpu.make_async_remote_copy(
            src_ref=src, dst_ref=dst, send_sem=ssem, recv_sem=rsem, device_id=dev, device_id_type=MESH
        )

    own = pl.ds(BLK, 2 * BLK)
    load_g = pltpu.make_async_copy(g_hbm, g_s, lsem.at[0])
    load_w = pltpu.make_async_copy(w_hbm, w_s, lsem.at[1])
    load_q = pltpu.make_async_copy(q_hbm, q_s, lsem.at[2])
    load_k = pltpu.make_async_copy(k_hbm, k_ext.at[own], lsem.at[3])
    load_v = pltpu.make_async_copy(v_hbm, v_ext.at[own], lsem.at[4])
    load_m = pltpu.make_async_copy(mask_hbm, mask, lsem.at[5])
    loads = [load_q, load_m, load_v, load_k, load_g, load_w]
    for copy in loads:
        copy.start()

    barrier = pltpu.get_barrier_semaphore()
    peers = [right, left] + x_peer + y_peer + z_peer
    for dev in peers:
        pl.semaphore_signal(barrier, inc=1, device_id=dev, device_id_type=MESH)

    pl.semaphore_wait(barrier, len(peers))

    first, last = pl.ds(0, BLK), pl.ds(BLK, BLK)
    low, high = pl.ds(0, BLK), pl.ds(3 * BLK, BLK)

    def halo_copy(n, g):
        c = pl.ds(g * GW, GW)
        src, dst = (k_hbm, k_ext) if n < 2 else (v_hbm, v_ext)
        if n % 2:
            return remote(src.at[first, c], dst.at[high, c], h_s.at[g, n], h_r.at[g, n], left)
        return remote(src.at[last, c], dst.at[low, c], h_s.at[g, n], h_r.at[g, n], right)

    def halo_send(g):
        for n in range(4):
            halo_copy(n, g).start()

    halo_send(0)

    def cols(g):
        return slice(g * GW, (g + 1) * GW)

    def rows_of(stat):
        return jnp.concatenate(
            [jnp.broadcast_to(stat[:, :BLK], (HD, BLK)), jnp.broadcast_to(stat[:, BLK:], (HD, BLK))], axis=0
        )

    load_q.wait()
    for b in range(2):
        for g in range(NG):
            scaled = q_s[b * BLK:(b + 1) * BLK, cols(g)] * jnp.asarray(HD ** -0.5, BF)
            qbd[b, g] = block_diag(scaled)
    load_m.wait()
    bias = []
    for b in range(2):
        row = ctx * 2 + b
        bias.append([jnp.where(mask[c, 0, row] == 1, 0.0, NEG).astype(F32) for c in (0, 2)])
    load_v.wait()
    v_t[:, BLK:3 * BLK] = v_ext[BLK:3 * BLK, :].T
    load_k.wait()

    def own_part(g):
        for b in range(2):
            s = nt(k_ext[BLK:3 * BLK, cols(g)], qbd[b, g])
            mid, other = s[b * BLK:(b + 1) * BLK], s[(1 - b) * BLK:(2 - b) * BLK]
            b_other = bias[b][1 - b]
            top = jnp.maximum(jnp.max(mid, axis=0, keepdims=True), jnp.max(other, axis=0, keepdims=True) + b_other)
            e_mid = jnp.exp(mid - top)
            e_other = jnp.exp(other - (top - b_other))
            total = jnp.sum(e_mid + e_other, axis=0, keepdims=True)
            pair = (e_mid, e_other) if b == 0 else (e_other, e_mid)
            e = jnp.concatenate(pair, axis=0).astype(BF)
            e_own[b, g] = e
            o_own[b, g] = diagonal(nn(v_t[cols(g), BLK:3 * BLK], e))
            stats[b, g, 0:1] = top
            stats[b, g, 1:2] = total

    def window(b):
        return slice(b * BLK, b * BLK + WIN)

    def halo_at(b):
        return slice(3 * b * BLK, 3 * b * BLK + BLK)

    def forward(g):
        parts = []
        for n in range(2):
            halo_copy(n, g).wait_recv()
        exps = []
        for b in range(2):
            s = nt(k_ext[halo_at(b), cols(g)], qbd[b, g])
            b_halo = bias[b][b]
            top_own = stats[b, g, 0:1]
            top = jnp.maximum(top_own, jnp.max(s, axis=0, keepdims=True) + b_halo)
            e = jnp.exp(s - (top - b_halo))
            shrink = jnp.exp(top_own - top)
            inv = 1.0 / (stats[b, g, 1:2] * shrink + jnp.sum(e, axis=0, keepdims=True))
            e = e.astype(BF)
            e_halo[b, g] = e
            stats[b, g, 2:3] = shrink * inv
            stats[b, g, 3:4] = inv
            exps.append((e, shrink * inv, inv))
        for n in range(2, 4):
            halo_copy(n, g).wait_recv()
        for b in range(2):
            e, f_own, f_halo = exps[b]
            o_halo = diagonal(nn(v_ext[halo_at(b), cols(g)].T, e))
            parts.append((o_own[b, g] * rows_of(f_own) + o_halo * rows_of(f_halo)).astype(BF))
        rows = jnp.concatenate(parts, axis=1)
        at[g] = rows.reshape(4, 2, 16, 2 * BLK)

    def core_copy(g):
        return remote(csend.at[g], crecv.at[g], c_s.at[g], c_r.at[g], mate)

    def x_copy(g, d):
        return remote(xsend.at[g, (x + d) % NX], xrecv.at[g, d - 1], x_s.at[g, d - 1], x_r.at[g, d - 1], x_peer[d - 1])

    def z_copy(g, side):
        t = side * ZL + g
        slot = (t + NZ - z) % NZ - 1
        return remote(zsend.at[g], zrecv.at[slot], z_s.at[g, side], z_r.at[slot], ident(y, t, x, core))

    def z_arrival(slot):
        return remote(zsend.at[0], zrecv.at[slot], z_s.at[0, 0], z_r.at[slot], z_peer[slot])

    def z_each(g, act):
        for side in range(ZH):
            @pl.when(z != side * ZL + g)
            def _():
                act(z_copy(g, side))

    def y_copy(j):
        slot = (j + NY - y) % NY - 1
        return remote(ysend, yrecv.at[slot], y_s.at[slot], y_r.at[slot], ident(j, z, x, core))

    def y_arrival(d):
        return remote(ysend, yrecv.at[d - 1], y_s.at[d - 1], y_r.at[d - 1], y_peer[d - 1])

    def y_each(act):
        for j in range(NY):
            @pl.when(y != j)
            def _():
                act(y_copy(j))

    def weight_part(g):
        mine = at[g, :, core].reshape(64, 2 * BLK)
        other = at[g, :, 1 - core].reshape(64, 2 * BLK)
        part = nn(jnp.concatenate([mine, other], axis=0), g_s[...])
        csend[g] = part[64:].astype(BF)
        dw_own[g] = part[:64]
        core_copy(g).start()

    def core_sum(g):
        core_copy(g).wait_recv()
        total = dw_own[g] + crecv[g].astype(F32)
        xsend[g] = total.astype(BF).reshape(4, 16, 1024)
        for d in sorted(range(1, NX), key=lambda d: -min(d, NX - d)):
            x_copy(g, d).start()

    def x_sum(g):
        total = xsend[g, x].astype(F32)
        for d in range(1, NX):
            x_copy(g, d).wait_recv()
            total += xrecv[g, d - 1].astype(F32)
        zsend[g] = total.astype(BF)
        z_each(g, lambda copy: copy.start())

    def z_sum(g):
        @pl.when(z % ZL == g)
        def _():
            total = zsend[g].astype(F32)
            for slot in range(NZ - 1):
                z_arrival(slot).wait_recv()
                total += zrecv[slot].astype(F32)
            ysend[...] = total.astype(BF)
            y_each(lambda copy: copy.start())

    def y_sum():
        total = ysend[...].astype(F32)
        for d in range(1, NY):
            y_arrival(d).wait_recv()
            total += yrecv[d - 1].astype(F32)
        dw_s[...] = total * wscale

    def grad_copy(side, g):
        return remote(gsend.at[side, g], grecv.at[side, g], g_ss.at[side, g], g_rs.at[side, g], right if side else left)

    def backward(g):
        tok = [slice(0, BLK), slice(BLK, 2 * BLK)]
        k_win, v_win = [], []
        rows = at[g].reshape(GW, 2 * BLK)
        q_parts = []
        for b in range(2):
            prod = rows[:, tok[b]].astype(F32) * da_t[cols(g), tok[b]].astype(F32)
            delta = jnp.concatenate(
                [jnp.sum(prod[:HD], axis=0, keepdims=True), jnp.sum(prod[HD:], axis=0, keepdims=True)], axis=1
            )
            dp_t = nt(v_ext[window(b), cols(g)], abd[b, g])
            p_own = e_own[b, g].astype(F32) * stats[b, g, 2:3]
            p_halo = e_halo[b, g].astype(F32) * stats[b, g, 3:4]
            p_all = jnp.concatenate((p_halo, p_own) if b == 0 else (p_own, p_halo), axis=0)
            p = p_all.astype(BF)
            ds = (p_all * (dp_t - delta)).astype(BF)
            v_win.append(nn(p, abd[b, g]))
            k_win.append(nn(ds, qbd[b, g]))
            q_parts.append((diagonal(nn(k_t[cols(g), window(b)], ds)) * (HD ** -0.5)).astype(BF))
        for n, win in enumerate((k_win, v_win)):
            gsend[0, g, n] = win[0][:BLK].astype(BF)
            gsend[1, g, n] = win[1][2 * BLK:].astype(BF)
        dk_acc[g] = k_win[0][BLK:] + k_win[1][:2 * BLK]
        dv_acc[g] = v_win[0][BLK:] + v_win[1][:2 * BLK]
        dq_t[cols(g), :] = jnp.concatenate(q_parts, axis=1)

    own_part(0)
    halo_send(1)
    own_part(1)
    halo_send(2)
    halo_send(3)
    own_part(2)
    load_g.wait()
    forward(0)
    weight_part(0)
    own_part(3)
    forward(1)
    weight_part(1)
    core_sum(0)
    forward(2)
    weight_part(2)
    core_sum(1)
    forward(3)
    weight_part(3)
    core_sum(2)
    load_w.wait()
    da = nt(g_s[...], w_s[...]).astype(BF)
    for b in range(2):
        for g in range(NG):
            abd[b, g] = block_diag(da[b * BLK:(b + 1) * BLK, cols(g)])
    core_sum(3)
    da_t[...] = nt(w_s[...], g_s[...]).astype(BF)
    k_t[...] = k_ext[...].T
    x_sum(0)
    backward(0)
    x_sum(1)
    backward(1)
    x_sum(2)
    x_sum(3)
    backward(2)
    z_sum(0)
    backward(3)
    for g in range(NG):
        grad_copy(0, g).start()
        grad_copy(1, g).start()
    z_sum(1)
    attn = at[...].reshape(NG * GW, 2 * BLK).T
    out_s[...] = nn(attn, w_s[...]).astype(BF)
    z_sum(2)
    dq_s[...] = dq_t[...].T
    z_sum(3)

    for g in range(NG):
        grad_copy(0, g).wait_recv()
        grad_copy(1, g).wait_recv()
        for n, (acc, dst) in enumerate(((dk_acc, dk_s), (dv_acc, dv_s))):
            dst[:BLK, cols(g)] = (acc[g, :BLK] + grecv[1, g, n].astype(F32)).astype(BF)
            dst[BLK:, cols(g)] = (acc[g, BLK:] + grecv[0, g, n].astype(F32)).astype(BF)
    for g in range(NG):
        for n in range(4):
            halo_copy(n, g).wait_send()
        core_copy(g).wait_send()
        for d in range(1, NX):
            x_copy(g, d).wait_send()
        z_each(g, lambda copy: copy.wait_send())
        grad_copy(0, g).wait_send()
        grad_copy(1, g).wait_send()
    y_sum()
    y_each(lambda copy: copy.wait_send())


def store_kernel(*refs):
    srcs, dsts, sem = refs[:5], refs[5:10], refs[10]
    copies = [pltpu.make_async_copy(src, dst, sem.at[n]) for n, (src, dst) in enumerate(zip(srcs, dsts))]
    for copy in copies:
        copy.start()
    for copy in copies:
        copy.wait()


def pinned(array, space):
    return pltpu.with_memory_space_constraint(array, space)


def body(dims, wscale, queries, keys, values, out_grad, w_out, block_mask):
    NY, ZH, ZL, NX = dims
    NZ = ZL * ZH
    tok, feat = queries.shape[1:]
    width = w_out.shape[1]
    free = pl.BlockSpec(memory_space=pl.ANY)
    vm = pltpu.VMEM
    dma = pltpu.SemaphoreType.DMA
    nx, ny, nz = max(NX - 1, 1), max(NY - 1, 1), max(NZ - 1, 1)
    shapes = (
        jax.ShapeDtypeStruct((tok, width), BF),
        jax.ShapeDtypeStruct((tok, feat), BF),
        jax.ShapeDtypeStruct((tok, feat), BF),
        jax.ShapeDtypeStruct((tok, feat), BF),
        jax.ShapeDtypeStruct((16, width), F32),
    )
    mask = jnp.transpose(block_mask, (2, 0, 1))
    arrays = [pinned(a, pltpu.HBM) for a in (queries[0], keys[0], values[0], out_grad[0], w_out, mask)]
    outs = pl.pallas_call(
        functools.partial(kernel, dims, wscale),
        out_shape=tuple(vm(a.shape, a.dtype) for a in shapes),
        in_specs=[free] * 6,
        out_specs=[pl.BlockSpec(memory_space=vm)] * 5,
        scratch_shapes=[
            pltpu.SMEM((block_mask.shape[2], 1, block_mask.shape[1]), jnp.int32),
            vm((tok, feat), BF),
            vm((4 * BLK, feat), BF),
            vm((4 * BLK, feat), BF),
            vm((tok, width), BF),
            vm((feat, width), BF),
            vm((feat, 4 * BLK), BF),
            vm((feat, 4 * BLK), BF),
            vm((feat, tok), BF),
            vm((2, NG, 2 * BLK, GW), BF),
            vm((2, NG, 2 * BLK, GW), BF),
            vm((2, NG, 2 * BLK, 2 * BLK), BF),
            vm((2, NG, BLK, 2 * BLK), BF),
            vm((2, NG, GW, BLK), F32),
            vm((2, NG, 8, 2 * BLK), F32),
            vm((NG, 4, 2, 16, tok), BF),
            vm((NG, 64, width), F32),
            vm((NG, 64, width), BF),
            vm((NG, 64, width), BF),
            vm((NG, 4, 16, width), BF),
            vm((NG, nx, 16, width), BF),
            vm((NG, 16, width), BF),
            vm((nz, 16, width), BF),
            vm((16, width), BF),
            vm((ny, 16, width), BF),
            vm((NG, tok, GW), F32),
            vm((NG, tok, GW), F32),
            vm((2, NG, 2, BLK, GW), BF),
            vm((2, NG, 2, BLK, GW), BF),
            vm((feat, tok), BF),
            dma((6,)),
            dma((NG, 4)), dma((NG, 4)),
            dma((NG,)), dma((NG,)),
            dma((NG, nx)), dma((NG, nx)),
            dma((NG, 2)), dma((nz,)),
            dma((ny,)), dma((ny,)),
            dma((2, NG)), dma((2, NG)),
        ],
        compiler_params=pltpu.CompilerParams(
            collective_id=0, has_side_effects=True, vmem_limit_bytes=40 * 1024 * 1024
        ),
    )(*arrays)
    outs = pl.pallas_call(
        store_kernel,
        out_shape=shapes,
        in_specs=[pl.BlockSpec(memory_space=vm)] * 5,
        out_specs=[free] * 5,
        scratch_shapes=[dma((5,))],
    )(*[pinned(a, vm) for a in outs])
    return (outs[0][None], outs[1][None], outs[2][None], outs[3][None], outs[4])


def solution(mesh, dims=(8, 2, 4, 4)):
    tokens = mesh.shape["dp"] * mesh.shape["ctx"] * 256
    placed = (
        P("dp", "ctx", None),
        P("dp", "ctx", None),
        P("dp", "ctx", None),
        P("dp", "ctx", None),
        P(),
        P("dp", None, None),
    )
    return jax.shard_map(
        functools.partial(body, dims, tokens ** -0.5),
        mesh=mesh,
        in_specs=placed,
        out_specs=(
            P("dp", "ctx", None),
            P("dp", "ctx", None),
            P("dp", "ctx", None),
            P("dp", "ctx", None),
            P("ctx", None),
        ),
        check_vma=False,
    )
```
